256 devices in a mesh: dp: 8 (over z), seq: 4 (over x), mp: 8 (over y, core).
Axes of the slice: x: 4, y: 4, z: 8, core: 2. Of those that a mesh axis runs over, the one named last changes fastest.
Arguments:
- hidden: bfloat16 [8, 1024, 8192], P('dp', 'seq'), may hold values from -6 to 6
- norm_gain: float32 [8192], replicated, may hold values from 0.5 to 1.5
- w_query: bfloat16 [8192, 4096], P(('dp', 'seq'), 'mp'), may hold values from -0.0625 to 0.0625
- w_key: bfloat16 [1280, 4096], P(None, 'mp'), may hold values from -0.15625 to 0.15625
- w_value: bfloat16 [1280, 4096], P(None, 'mp'), may hold values from -0.15625 to 0.15625
- w_out: bfloat16 [4096, 8192], P('mp', ('dp', 'seq')), may hold values from -0.375 to 0.375
- gate_alpha: float32 [8192], P('mp'), may hold values from 0.3 to 1.5
- latents: bfloat16 [128, 64, 1280], P(('dp', 'seq')), may hold values from -410 to 410
- image_doc: int32 [128, 1], replicated, may hold values from 0 to 7; in each aligned block of 4 rows (0 to 3, 4 to 7, ...) at most 2 rows name the same one
- image_pos: int32 [128], replicated, may hold values from 0 to 1023
Outputs:
- cross_out: bfloat16 [8, 1024, 8192], P('dp', 'seq', 'mp')
The draws below stay inside these ranges and needn't reach their ends.
Inputs may be any that keep to these rules, and one draw needn't show every extreme that they name: `image_doc`: in the rows of one device (aligned blocks of 4 images) at most 2 images belong to one document, and some block of every draw has exactly 2; every document has an image.
All inputs are finite; a program needn't handle non-finite values.
Results may differ from the reference program's by a relative error of at most 0.02.
The reference program's roundings to bfloat16 on the way count: a program that leaves them out, or rounds other values in their place, can miss the bound.
Values may be sent and summed in bfloat16 or wider, within the bound.
A program may use at most 128 MiB of HBM per device.

```python
import math
import jax
import jax.numpy as jnp
import numpy as np
from jax import lax

D = 8192
HEADS = 32
HEAD_DIM = 128
LW = 1280
NLAT = 64
IMG_DEV = 4
CAP = 2
L = 1024
DOCS = 8
IMAGES = 128
N_MP = 8


def draw_latents(key, part):
    key = jax.random.fold_in(key, 7)
    base_key = jax.random.fold_in(key, 0)
    return jnp.clip(jax.random.normal(base_key, (IMAGES, NLAT, LW), jnp.float32), -6.0, 6.0).astype(jnp.bfloat16)


def touch_ends(entries, key, smallest, high):
    extent = entries.shape
    place = [jax.random.randint(jax.random.fold_in(key, axis), (), 0, extent[axis]) for axis in range(len(extent))]
    entries = entries.at[tuple(place)].set(smallest)
    longest = extent.index(max(extent))
    place[longest] = (place[longest] + 1) % extent[longest]
    return entries.at[tuple(place)].set(high)


def steps_of(own_key, shape, shards, low, top_value):
    factor_of, own = 1.0, jax.random.fold_in(own_key, 6)
    for axis_at, parts in shards:
        draws = jnp.exp(jax.random.uniform(jax.random.fold_in(own, axis_at), (parts,), jnp.float32, low / len(shards), top_value / len(shards)))
        factor_of = factor_of * jnp.repeat(draws, shape[axis_at] // parts).reshape([-1 if axis == axis_at else 1 for axis in range(len(shape))])
    return factor_of


def deal_out(rng, own, number, rows, number_of, top, bound, lean):
    order = jax.random.permutation(rng, number_of)
    heavy_load, common = load_shares(number_of, rows * top, bound, lean, True), load_shares(number_of, rows * top, bound, lean, False)
    places = jnp.arange(number_of)

    def named(lengths, offset_by):
        used = int((lengths > 0).sum())
        fixed = max(1, used // 4)
        passed = fixed + (places - fixed + offset_by * (used - fixed)) % max(1, number_of - fixed)
        return jnp.zeros((number_of,), jnp.int32).at[order[jnp.where(places < fixed, places, passed)]].set(jnp.asarray(lengths, jnp.int32))

    lengths = jnp.where(number % 4 == 0, named(heavy_load, number // 4), named(common, number - number // 4 - 1))
    mixed = jax.random.permutation(jax.random.fold_in(own, 3), number_of)
    donor, receiver = mixed[0:number_of // 2 * 2:2], mixed[1:number_of // 2 * 2:2]
    room = jnp.minimum(lengths[donor] - 1, bound - lengths[receiver]) // 2
    room = jnp.where((donor == order[0]) | (receiver == order[0]) | (lengths[receiver] == 0), 0, jnp.maximum(room, 0))
    passed = jax.random.randint(jax.random.fold_in(own, 4), (number_of // 2,), 0, 1 << 20) % (room + 1)
    lengths = lengths.at[donor].add(-passed).at[receiver].add(passed)
    items = jnp.searchsorted(jnp.cumsum(lengths), jnp.arange(rows * top), side="right").astype(jnp.int32)
    listing = items.reshape(top, rows).T
    listing = listing[jax.random.permutation(jax.random.fold_in(own, 1), rows)]
    offset_by = jax.random.randint(jax.random.fold_in(own, 2), (rows, 1), 0, top)
    return jnp.take_along_axis(listing, (jnp.arange(top)[None, :] + offset_by) % top, axis=1)


def load_shares(number_of, total, reach, slope, full):
    loads = [(1 << 20) // math.isqrt(rank ** slope) + 1 for rank in range(1, number_of + 1)]
    largest = reach if full else min(reach, max(-(-total // number_of), total * loads[0] // sum(loads)))
    least = 1 if total - largest >= number_of - 1 else 0
    holding, spare = [largest] + [least] * (number_of - 1), total - largest - least * (number_of - 1)
    while spare > 0:
        free = [i for i in range(1, number_of) if holding[i] < largest] or [i for i in range(1, number_of) if holding[i] < reach]
        pool, budget = sum([loads[i] for i in free]), spare
        for i in free:
            addition = min(reach - holding[i], max(1, budget * loads[i] // pool), spare)
            holding[i] = holding[i] + addition
            spare = spare - addition
    return np.array(holding)


def noise(rng, dims, scale, most, cuts=(), kind=jnp.bfloat16):
    values = jax.random.normal(rng, dims, jnp.float32) * scale
    if len(cuts) > 0:
        values = steps_of(rng, dims, cuts, -0.22, 0.18) * values
    return jnp.clip(values, min=-most, max=most).astype(kind)


def setup_inputs(seed: int = 0) -> dict:
    keys = jax.random.split(jax.random.key(seed), 11)
    hidden = noise(keys[0], (DOCS, L, D), 1.0, 6.0, ((0, 8), (1, 4)))
    norm_gain = jnp.clip(1.0 + 0.1 * jax.random.normal(keys[1], (D,), jnp.float32), 0.5, 1.5)
    w_query = noise(keys[2], (D, HEADS * HEAD_DIM), D ** -0.5, 0.0625, ((0, 32), (1, 8)))
    w_key = noise(keys[3], (LW, HEADS * HEAD_DIM), LW ** -0.5, 0.15625, ((1, 8),))
    w_value = noise(keys[4], (LW, HEADS * HEAD_DIM), LW ** -0.5, 0.15625, ((1, 8),))
    w_out = noise(keys[5], (HEADS * HEAD_DIM, D), (HEADS * HEAD_DIM // 16) ** -0.5, 0.375, ((0, 8), (1, 32)))
    gate_alpha = jnp.clip(0.3 + 1.2 * jax.random.uniform(keys[6], (D,), jnp.float32) ** steps_of(keys[6], (D,), ((0, 8),), -0.2, 0.2), 0.3, 1.5)
    latents = draw_latents(jax.random.fold_in(keys[10], 71), 0)
    image_doc_keys = jax.random.split(jax.random.fold_in(keys[8], 1), IMAGES // IMG_DEV)
    image_doc_turns = jax.random.permutation(jax.random.fold_in(keys[8], 3), IMAGES // IMG_DEV)
    image_doc = jax.vmap(lambda own, number: deal_out(jax.random.fold_in(keys[8], 2), own, number, IMG_DEV, DOCS, 1, CAP, 2))(image_doc_keys, image_doc_turns).reshape((IMAGES, 1))
    image_pos = touch_ends(jax.random.randint(keys[9], (IMAGES,), 0, L), jax.random.fold_in(keys[9], 1), 0, L - 1).astype(jnp.int32)
    return dict(hidden=hidden, norm_gain=norm_gain, w_query=w_query, w_key=w_key, w_value=w_value, w_out=w_out, gate_alpha=gate_alpha, latents=latents, image_doc=image_doc, image_pos=image_pos)


epsilon = 1e-05

def reference(hidden, norm_gain, w_query, w_key, w_value, w_out, gate_alpha, latents, image_doc, image_pos):
    score_scale = HEAD_DIM ** (-0.5)
    widened = hidden.astype(jnp.float32)
    normed = (widened * lax.rsqrt(lax.optimization_barrier(jnp.mean(widened * widened, axis=-1, keepdims=True)) + epsilon) * norm_gain).astype(jnp.bfloat16)
    lat_rows = latents.reshape(IMAGES * NLAT, LW)
    key_rows = jnp.dot(lat_rows, w_key, preferred_element_type=jnp.float32).astype(jnp.bfloat16)
    value_rows = jnp.dot(lat_rows, w_value, preferred_element_type=jnp.float32).astype(jnp.bfloat16)
    key_heads = jnp.transpose(key_rows.reshape(IMAGES * NLAT, HEADS, HEAD_DIM), (1, 0, 2))
    value_heads = jnp.transpose(value_rows.reshape(IMAGES * NLAT, HEADS, HEAD_DIM), (1, 0, 2))
    key_doc = jnp.repeat(image_doc[:, 0], NLAT)
    key_pos = jnp.repeat(image_pos, NLAT)
    text_pos = jnp.arange(L, dtype=jnp.int32)
    gate_value = jnp.tanh(gate_alpha)
    group_width = HEADS * HEAD_DIM // N_MP

    def one_doc(inputs):
        doc_rows, doc_index = inputs
        queries = jnp.dot(doc_rows, w_query, preferred_element_type=jnp.float32).astype(jnp.bfloat16)
        query_heads = jnp.transpose(queries.reshape(L, HEADS, HEAD_DIM), (1, 0, 2))
        visible = (key_doc[None, :] == doc_index) & (key_pos[None, :] <= text_pos[:, None])
        present = jnp.any(visible, axis=1)

        def one_head(operands):
            query_one, key_one, value_one = operands
            scores = jnp.dot(query_one, key_one.T, preferred_element_type=jnp.float32) * score_scale
            scores = jnp.where(visible, scores, -1e+30)
            row_max = lax.optimization_barrier(jnp.max(scores, axis=-1, keepdims=True))
            weights = jnp.exp(scores - row_max)
            running = lax.optimization_barrier(jnp.sum(weights, axis=-1, keepdims=True))
            mixed = jnp.dot(weights.astype(jnp.bfloat16), value_one, preferred_element_type=jnp.float32) / running
            return mixed.astype(jnp.bfloat16)
        head_out = lax.map(one_head, (query_heads, key_heads, value_heads))
        attended = jnp.transpose(head_out, (1, 0, 2)).reshape(L, HEADS * HEAD_DIM)
        summed = jnp.zeros((L, D), jnp.float32)
        for group in range(N_MP):
            partial_value = jnp.dot(attended[:, group * group_width:(group + 1) * group_width], w_out[group * group_width:(group + 1) * group_width], preferred_element_type=jnp.float32).astype(jnp.bfloat16)
            summed = summed + lax.optimization_barrier(partial_value).astype(jnp.float32)
        return (summed * gate_value * present[:, None].astype(jnp.float32)).astype(jnp.bfloat16)
    return lax.map(one_doc, (normed, jnp.arange(DOCS, dtype=jnp.int32)))
```

```python
import functools

import jax
import jax.numpy as jnp
from jax import lax
from jax.experimental import pallas as pl
from jax.experimental.pallas import tpu as pltpu
from jax.sharding import PartitionSpec as P

HEAD_DIM = 128
EPSILON = 1e-05
NZ, NX, NM, NY = 8, 4, 8, 4
LOG2E = 1.4426950408889634
MASKED = -1e30
FAR = 1 << 20
BF16, F32 = jnp.bfloat16, jnp.float32


def dot(a, b):
    return jnp.dot(a, b, preferred_element_type=F32)


def kernel(
    hidden, gain, w_query, w_key, w_value, w_out, gate, latents, doc_ref, pos_ref,
    out,
    hid_v, lat_v, wk_v, wv_v, lat_out, lat_all, norm_out, norm_all, wq_all, wo_all,
    kv_out, kv_all, key_pos, q_out, q_in, scores, att_all,
    pair_out, pair_own, pair_in, sum_out, sum_in, fin_out,
    send_sems, recv_sems, local_sems,
):
    z, x, m = lax.axis_index("dp"), lax.axis_index("seq"), lax.axis_index("mp")
    y, c = m // 2, lax.rem(m, 2)
    sibling = (z, x, m + 1 - 2 * c)

    def at_z(off):
        return (lax.rem(z + off + NZ, NZ), x, m)

    def at_x(off):
        return (z, lax.rem(x + off, NX), m)

    def at_y(off):
        return (z, x, lax.rem(m + 2 * off, NM))

    taken = [0]
    sent = []

    def remote(src, dst, device):
        slot = taken[0]
        taken[0] += 1
        return pltpu.make_async_remote_copy(
            src_ref=src, dst_ref=dst, send_sem=send_sems.at[slot], recv_sem=recv_sems.at[slot],
            device_id=device, device_id_type=pl.DeviceIdType.MESH,
        )

    def start(copy):
        copy.start()
        sent.append(copy)

    tok_part = pl.ds(pl.multiple_of(m * 32, 32), 32)
    lat_part = pl.ds(pl.multiple_of(lax.rem(m, 4) * 16, 16), 16)
    loads = [
        pltpu.make_async_copy(s, d, local_sems.at[i])
        for i, (s, d) in enumerate((
            (latents.at[:, lat_part, :], lat_v),
            (hidden.at[0, tok_part, :], hid_v),
            (w_key, wk_v),
            (w_value, wv_v),
            (w_query, wq_all.at[z]),
            (w_out, wo_all.at[z]),
        ))
    ]
    for load in loads:
        load.start()

    partners = [at_z(o) for o in range(1, NZ)] + [at_x(o) for o in range(1, NX)]
    partners += [at_y(o) for o in range(1, NY)] + [sibling]
    barrier = pltpu.get_barrier_semaphore()
    for partner in partners:
        pl.semaphore_signal(
            barrier, inc=1, device_id=partner, device_id_type=pl.DeviceIdType.MESH
        )
    pl.semaphore_wait(barrier, len(partners))

    def make_ring(own, buf):
        half = own.shape[0] // 2
        steps = []
        for s in range(4):
            up_from, down_from = lax.rem(z - s + NZ, NZ), lax.rem(z + s, NZ)
            up, down = buf.at[up_from], buf.at[down_from]
            if s == 3:
                up, down = buf.at[up_from, pl.ds(0, half)], buf.at[down_from, pl.ds(half, half)]
            steps.append((
                remote(own if s == 0 else up, up, at_z(1)),
                remote(own if s == 0 else down, down, at_z(-1)),
            ))
        return steps

    ring_q = make_ring(w_query, wq_all)
    ring_o = make_ring(w_out, wo_all)

    def ring_start(ring, s):
        if s > 0:
            ring_wait(ring, s - 1)
        for copy in ring[s]:
            start(copy)

    def ring_wait(ring, s):
        for copy in ring[s]:
            copy.wait_recv()

    base = (z * NX + x) * 4
    docs = [doc_ref[0, base + i] for i in range(4)]
    ranks = []
    for i in range(4):
        rank = jnp.int32(0)
        for before in range(i):
            rank = rank + jnp.where(docs[before] == docs[i], 1, 0)
        ranks.append(rank)
    slot_here = m // 4
    loads[0].wait()

    def route(doc, carry):
        total = None
        for i in range(4):
            chosen = (docs[i] == doc) & (ranks[i] == slot_here)
            term = lat_v[i].astype(F32) * jnp.where(chosen, 1.0, 0.0).astype(F32)
            total = term if total is None else total + term
        lat_out[doc] = total.astype(BF16)
        return carry

    lax.fori_loop(0, NZ, route, 0)
    lat_z = []
    for o in range(1, NZ):
        target = at_z(o)
        copy = remote(lat_out.at[target[0]], lat_all.at[m, z], target)
        start(copy)
        lat_z.append(copy)
    lat_all[m, z] = lat_out[z]
    ring_start(ring_q, 0)

    loads[1].wait()

    def square_sum(i, total):
        part = hid_v[:, pl.ds(pl.multiple_of(i * 1024, 1024), 1024)].astype(F32)
        return total + jnp.sum(part * part, axis=-1, keepdims=True)

    mean_square = lax.fori_loop(0, 8, square_sum, jnp.zeros((32, 1), F32)) / 8192.0
    inverse = lax.rsqrt(mean_square + EPSILON)

    def normalise(i, carry):
        cols = pl.ds(pl.multiple_of(i * 1024, 1024), 1024)
        rows = (hid_v[:, cols].astype(F32) * inverse * gain[:, cols]).astype(BF16)
        for owner in range(NX):
            norm_out[owner, :, pl.ds(pl.multiple_of(i * 256, 256), 256)] = rows[
                :, owner * 256 : owner * 256 + 256
            ]
        return carry

    lax.fori_loop(0, 8, normalise, 0)
    hid_x = []
    for o in (1, 3, 2):
        target = at_x(o)
        copy = remote(norm_out.at[target[1]], norm_all.at[x, m], target)
        start(copy)
        hid_x.append(copy)
    norm_all[x, m] = norm_out[x]

    lane_owner = lax.broadcasted_iota(jnp.int32, (1, 128), 1) // 16

    def positions(source_z, first):
        for source_x in range(NX):
            block = (source_z * NX + source_x) * 4
            slot_pos = [jnp.int32(FAR), jnp.int32(FAR)]
            seen = jnp.int32(0)
            for i in range(4):
                match = doc_ref[0, block + i] == z
                place = pos_ref[0, block + i]
                for r in range(2):
                    slot_pos[r] = jnp.where(match & (seen == r), place, slot_pos[r])
                seen = seen + jnp.where(match, 1, 0)
            for r in range(2):
                key_pos[source_x * 2 + r] = jnp.where(
                    lane_owner == source_z, slot_pos[r], key_pos[source_x * 2 + r]
                )
                first = jnp.minimum(first, slot_pos[r])
        return first

    key_pos[...] = jnp.full(key_pos.shape, FAR, jnp.int32)
    first_pos = lax.fori_loop(0, NZ, positions, jnp.int32(FAR))

    def make_gather(buf):
        along, across = {}, {}
        for o in (1, 3, 2):
            along[o] = remote(buf(m), buf(m), at_y(o))
        across[0] = remote(buf(m), buf(m), sibling)
        for o in (1, 3, 2):
            came = lax.rem(m - 2 * o + NM, NM)
            across[o] = remote(buf(came), buf(came), sibling)
        return along, across

    def gather_start(gather):
        along, across = gather
        for o in (1, 3, 2):
            start(along[o])
        start(across[0])

    def gather_pass(gather, o):
        along, across = gather
        along[o].wait_recv()
        start(across[o])

    lat_gather = make_gather(lambda who: lat_all.at[who])
    hid_gather = [make_gather(lambda who, k=k: norm_all.at[k, who]) for k in range(NX)]

    ring_start(ring_q, 1)
    for copy in lat_z:
        copy.wait_recv()
    gather_start(lat_gather)

    for copy in hid_x:
        copy.wait_recv()
    for k in range(NX):
        gather_start(hid_gather[k])

    kv_sends = []

    def keys_values(o):
        chip = lax.rem(y - o + NY, NY)
        rows = lat_all[pl.ds(chip * 2, 2)].reshape(256, 1280)
        for weight, at in ((wk_v, 0), (wv_v, HEAD_DIM)):
            made = dot(rows, weight[...]).astype(BF16)
            for head in range(NX):
                kv_out[head, chip, :, at : at + HEAD_DIM] = made[
                    :, head * HEAD_DIM : (head + 1) * HEAD_DIM
                ]
        for off in (1, 3, 2):
            target = at_x(off)
            copy = remote(kv_out.at[target[1], chip], kv_all.at[x, chip], target)
            start(copy)
            kv_sends.append(copy)
        kv_all[x, chip] = kv_out[x, chip]

    loads[2].wait()
    loads[3].wait()
    lat_gather[1][0].wait_recv()
    keys_values(0)
    ring_start(ring_q, 2)
    for o in (1, 3, 2):
        gather_pass(lat_gather, o)
        lat_gather[1][o].wait_recv()
        keys_values(o)
        if o == 3:
            ring_start(ring_q, 3)

    ring_wait(ring_q, 3)
    ring_start(ring_o, 0)
    loads[4].wait()
    q_sends = []
    for k in range(NX):
        for o in (1, 3, 2):
            gather_pass(hid_gather[k], o)
        for o in (0, 1, 3, 2):
            hid_gather[k][1][o].wait_recv()
        made = dot(norm_all[k].reshape(256, 2048), wq_all[...].reshape(2048, 512))
        for head in range(NX):
            q_out[k, head] = made[:, head * HEAD_DIM : (head + 1) * HEAD_DIM]
        copies = []
        for off in (1, 3, 2):
            target = at_x(off)
            copy = remote(q_out.at[k, target[1]], q_in.at[k, x], target)
            start(copy)
            copies.append(copy)
        q_sends.append(copies)
        if k < 3:
            ring_start(ring_o, k + 1)

    for copy in kv_sends:
        copy.wait_recv()

    head_lanes = pl.ds(pl.multiple_of(x * HEAD_DIM, HEAD_DIM), HEAD_DIM)
    att_sends = {}

    def attend(k):
        for copy in q_sends[k]:
            copy.wait_recv()
        query = q_out[k, x]
        for off in (1, 3, 2):
            query = query + q_in[k, lax.rem(x - off + NX, NX)]
        query = query.astype(BF16)
        text_pos = lax.broadcasted_iota(jnp.int32, (256, 128), 0) + k * 256

        def score(i, top):
            block = kv_all[i // 2, pl.ds(lax.rem(i, 2) * 2, 2)].reshape(512, 256)
            raw = lax.dot_general(
                query, block[:, :HEAD_DIM], (((1,), (1,)), ((), ())), preferred_element_type=F32
            )
            visible = key_pos[i] <= text_pos
            for g in range(4):
                part = jnp.where(visible, raw[:, g * 128 : (g + 1) * 128], MASKED)
                scores[i, :, g * 128 : (g + 1) * 128] = part
                top = jnp.maximum(top, part)
            return top

        top = lax.fori_loop(0, 8, score, jnp.full((256, 128), MASKED, F32))
        row_max = jnp.max(top, axis=-1, keepdims=True)

        def mix(i, carry):
            mixed, running = carry
            weights = jnp.exp2((scores[i] - row_max) * (HEAD_DIM ** (-0.5) * LOG2E))
            for g in range(4):
                running = running + weights[:, g * 128 : (g + 1) * 128]
            block = kv_all[i // 2, pl.ds(lax.rem(i, 2) * 2, 2)].reshape(512, 256)
            return mixed + dot(weights.astype(BF16), block[:, HEAD_DIM:]), running

        zero = jnp.zeros((256, 128), F32)
        mixed, running = lax.fori_loop(0, 8, mix, (zero, zero))
        att_all[k, :, head_lanes] = (
            mixed / jnp.sum(running, axis=-1, keepdims=True)
        ).astype(BF16)
        copies = []
        for off in (1, 3, 2):
            copy = remote(att_all.at[k, :, head_lanes], att_all.at[k, :, head_lanes], at_x(off))
            start(copy)
            copies.append(copy)
        att_sends[k] = copies

    pair_sends, sum_sends = {}, {}

    def project(k):
        for copy in att_sends[k]:
            copy.wait_recv()
        rows = att_all[k]

        def other(i, carry):
            pair_out[k, i] = dot(rows, wo_all[2 * i + 1 - c]).astype(BF16)
            return carry

        lax.fori_loop(0, NY, other, 0)
        pair = remote(pair_out.at[k], pair_in.at[k], sibling)
        start(pair)

        def mine(i, carry):
            pair_own[k, i] = dot(rows, wo_all[2 * i + c]).astype(BF16)
            return carry

        lax.fori_loop(0, NY, mine, 0)
        pair.wait_recv()
        copies = []
        for off in (1, 3, 2):
            to = lax.rem(y + off, NY)
            sum_out[k, to] = (
                pair_own[k, to].astype(F32) + pair_in[k, to].astype(F32)
            ).astype(BF16)
            copy = remote(sum_out.at[k, to], sum_in.at[k, y], at_y(off))
            start(copy)
            copies.append(copy)
        sum_sends[k] = copies

    out_cols = pl.ds(pl.multiple_of(x * 256, 256), 256)
    gate_here = jnp.tanh(gate[:, out_cols])
    fin_sends = []

    def finish(k):
        for copy in sum_sends[k]:
            copy.wait_recv()
        total = pair_own[k, y].astype(F32) + pair_in[k, y].astype(F32)
        for off in (1, 3, 2):
            total = total + sum_in[k, lax.rem(y - off + NY, NY)].astype(F32)
        present = lax.broadcasted_iota(jnp.int32, (256, 256), 0) + k * 256 >= first_pos
        result = total * gate_here * jnp.where(present, 1.0, 0.0)
        fin_out[k] = result.astype(BF16)
        copy = pltpu.make_async_remote_copy(
            src_ref=fin_out.at[k], dst_ref=out.at[0, :, out_cols],
            send_sem=send_sems.at[taken[0] + k], recv_sem=recv_sems.at[taken[0] + NX + x],
            device_id=(z, k, m), device_id_type=pl.DeviceIdType.MESH,
        )
        keep = pltpu.make_async_copy(fin_out.at[k], out.at[0, :, out_cols], local_sems.at[6])

        @pl.when(x == k)
        def _():
            keep.start()

        @pl.when(x != k)
        def _():
            copy.start()

        fin_sends.append((copy, keep))

    ring_wait(ring_o, 3)
    loads[5].wait()
    attend(0)
    attend(1)
    project(0)
    attend(2)
    project(1)
    attend(3)
    project(2)
    project(3)
    first_fin = taken[0]
    for k in range(NX):
        finish(k)

    for off in (1, 3, 2):
        source = lax.rem(x - off + NX, NX)
        cols = pl.ds(pl.multiple_of(source * 256, 256), 256)
        pltpu.make_async_remote_copy(
            src_ref=fin_out.at[0], dst_ref=out.at[0, :, cols],
            send_sem=send_sems.at[first_fin], recv_sem=recv_sems.at[first_fin + NX + source],
            device_id=at_x(off), device_id_type=pl.DeviceIdType.MESH,
        ).wait_recv()
    for k, (copy, keep) in enumerate(fin_sends):

        @pl.when(x == k)
        def _():
            keep.wait()

        @pl.when(x != k)
        def _():
            copy.wait_send()

    for copy in sent:
        copy.wait_send()


def on_device(
    hidden, norm_gain, w_query, w_key, w_value, w_out, gate_alpha, latents, image_doc, image_pos
):
    vmem = pl.BlockSpec(memory_space=pltpu.VMEM)
    smem = pl.BlockSpec(memory_space=pltpu.SMEM)
    anywhere = pl.BlockSpec(memory_space=pl.ANY)
    buffer = pltpu.VMEM
    return pl.pallas_call(
        kernel,
        out_shape=jax.ShapeDtypeStruct((1, 256, 1024), BF16),
        in_specs=[
            anywhere, vmem, anywhere, anywhere, anywhere, anywhere, vmem, anywhere, smem, smem,
        ],
        out_specs=anywhere,
        scratch_shapes=[
            buffer((32, 8192), BF16),
            buffer((4, 16, 1280), BF16),
            buffer((1280, 512), BF16),
            buffer((1280, 512), BF16),
            buffer((NZ, 16, 1280), BF16),
            buffer((NM, NZ, 16, 1280), BF16),
            buffer((NX, 32, 2048), BF16),
            buffer((NX, NM, 32, 2048), BF16),
            buffer((NZ, 256, 512), BF16),
            buffer((NZ, 512, 256), BF16),
            buffer((NX, NY, 256, 256), BF16),
            buffer((NX, NY, 256, 256), BF16),
            buffer((NX * 2, 1, 128), jnp.int32),
            buffer((NX, NX, 256, 128), F32),
            buffer((NX, NX, 256, 128), F32),
            buffer((8, 256, 512), F32),
            buffer((NX, 256, 512), BF16),
            buffer((NX, NY, 256, 256), BF16),
            buffer((NX, NY, 256, 256), BF16),
            buffer((NX, NY, 256, 256), BF16),
            buffer((NX, NY, 256, 256), BF16),
            buffer((NX, NY, 256, 256), BF16),
            buffer((NX, 256, 256), BF16),
            pltpu.SemaphoreType.DMA((160,)),
            pltpu.SemaphoreType.DMA((160,)),
            pltpu.SemaphoreType.DMA((8,)),
        ],
        compiler_params=pltpu.CompilerParams(
            collective_id=0, has_side_effects=True, vmem_limit_bytes=56 * 2**20
        ),
    )(
        hidden, norm_gain.reshape(1, -1), w_query, w_key, w_value, w_out,
        gate_alpha.reshape(1, -1), latents, image_doc.reshape(1, -1), image_pos.reshape(1, -1),
    )


def solution(mesh):
    placed = (
        P("dp", "seq", None),
        P(),
        P(("dp", "seq"), "mp"),
        P(None, "mp"),
        P(None, "mp"),
        P("mp", ("dp", "seq")),
        P("mp"),
        P(("dp", "seq"), None, None),
        P(),
        P(),
    )
    return jax.shard_map(
        on_device, mesh=mesh, in_specs=placed, out_specs=P("dp", "seq", "mp"), check_vma=False
    )
```

```python
import functools

import jax
import jax.numpy as jnp
from jax import lax
from jax.experimental import pallas as pl
from jax.experimental.pallas import tpu as pltpu
from jax.sharding import PartitionSpec as P

HEAD_DIM = 128
EPSILON = 1e-05
NZ, NX, NM, NY = 8, 4, 8, 4
LOG2E = 1.4426950408889634
MASKED = -1e30
FAR = 1 << 20
BF16, F32 = jnp.bfloat16, jnp.float32


def dot(a, b):
    return jnp.dot(a, b, preferred_element_type=F32)


def kernel(
    hidden, gain, w_query, w_key, w_value, w_out, gate, latents, doc_ref, pos_ref,
    out,
    hid_v, lat_v, wk_v, wv_v, lat_out, lat_all, norm_out, norm_all, wq_all, wo_all,
    kv_out, kv_all, key_pos, q_out, q_mid, q_in, scores, att_all,
    pair_out, pair_own, pair_in, sum_out, sum_mid, sum_in, fin_out,
    send_sems, recv_sems, local_sems,
):
    z, x, m = lax.axis_index("dp"), lax.axis_index("seq"), lax.axis_index("mp")
    y, c = m // 2, lax.rem(m, 2)
    sibling = (z, x, m + 1 - 2 * c)

    def at_z(off):
        return (lax.rem(z + off + NZ, NZ), x, m)

    def at_x(off):
        return (z, lax.rem(x + off, NX), m)

    def at_y(off):
        return (z, x, lax.rem(m + 2 * off, NM))

    taken = [0]
    sent = []

    def take(count):
        first = taken[0]
        taken[0] += count
        return first

    def remote(src, dst, device, slot=None):
        if slot is None:
            slot = take(1)
        return pltpu.make_async_remote_copy(
            src_ref=src, dst_ref=dst, send_sem=send_sems.at[slot], recv_sem=recv_sems.at[slot],
            device_id=device, device_id_type=pl.DeviceIdType.MESH,
        )

    def start(copy):
        copy.start()
        sent.append(copy)

    partners = [at_z(o) for o in range(1, NZ)] + [at_x(o) for o in range(1, NX)]
    partners += [at_y(o) for o in range(1, NY)] + [sibling]
    barrier = pltpu.get_barrier_semaphore()
    for partner in partners:
        pl.semaphore_signal(
            barrier, inc=1, device_id=partner, device_id_type=pl.DeviceIdType.MESH
        )

    tok_part = pl.ds(pl.multiple_of(m * 32, 32), 32)
    lat_part = pl.ds(pl.multiple_of(lax.rem(m, 4) * 16, 16), 16)
    loads = [
        pltpu.make_async_copy(s, d, local_sems.at[i])
        for i, (s, d) in enumerate((
            (latents.at[:, lat_part, :], lat_v),
            (hidden.at[0, tok_part, :], hid_v),
            (w_key, wk_v),
            (w_value, wv_v),
            (w_query, wq_all.at[z]),
            (w_out, wo_all.at[z]),
        ))
    ]
    for load in loads:
        load.start()

    def make_ring(own, buf):
        half = own.shape[0] // 2
        steps = []
        for s in range(4):
            up_from, down_from = lax.rem(z - s + NZ, NZ), lax.rem(z + s, NZ)
            up, down = buf.at[up_from], buf.at[down_from]
            if s == 3:
                up, down = buf.at[up_from, pl.ds(0, half)], buf.at[down_from, pl.ds(half, half)]
            steps.append((
                remote(own if s == 0 else up, up, at_z(1)),
                remote(own if s == 0 else down, down, at_z(-1)),
            ))
        return steps

    ring_q = make_ring(w_query, wq_all)
    ring_o = make_ring(w_out, wo_all)

    def ring_start(ring, s):
        if s > 0:
            ring_wait(ring, s - 1)
        for copy in ring[s]:
            start(copy)

    def ring_wait(ring, s):
        for copy in ring[s]:
            copy.wait_recv()

    base = (z * NX + x) * 4
    docs = [doc_ref[0, base + i] for i in range(4)]
    ranks = []
    for i in range(4):
        rank = jnp.int32(0)
        for before in range(i):
            rank = rank + jnp.where(docs[before] == docs[i], 1, 0)
        ranks.append(rank)
    slot_here = m // 4
    loads[0].wait()

    def route(doc, carry):
        total = None
        for i in range(4):
            chosen = (docs[i] == doc) & (ranks[i] == slot_here)
            term = lat_v[i].astype(F32) * jnp.where(chosen, 1.0, 0.0).astype(F32)
            total = term if total is None else total + term
        lat_out[doc] = total.astype(BF16)
        return carry

    lax.fori_loop(0, NZ, route, 0)
    pl.semaphore_wait(barrier, len(partners))
    lat_z = []
    for o in range(1, NZ):
        target = at_z(o)
        copy = remote(lat_out.at[target[0]], lat_all.at[m, z], target)
        start(copy)
        lat_z.append(copy)
    lat_all[m, z] = lat_out[z]

    loads[1].wait()

    def square_sum(i, total):
        part = hid_v[:, pl.ds(pl.multiple_of(i * 1024, 1024), 1024)].astype(F32)
        return total + jnp.sum(part * part, axis=-1, keepdims=True)

    mean_square = lax.fori_loop(0, 8, square_sum, jnp.zeros((32, 1), F32)) / 8192.0
    inverse = lax.rsqrt(mean_square + EPSILON)

    def normalise(i, carry):
        cols = pl.ds(pl.multiple_of(i * 1024, 1024), 1024)
        rows = (hid_v[:, cols].astype(F32) * inverse * gain[:, cols]).astype(BF16)
        for owner in range(NX):
            norm_out[owner, :, pl.ds(pl.multiple_of(i * 256, 256), 256)] = rows[
                :, owner * 256 : owner * 256 + 256
            ]
        return carry

    lax.fori_loop(0, 8, normalise, 0)
    hid_x_first = take(NX)
    for o in (1, 3, 2):
        target = at_x(o)
        start(remote(norm_out.at[target[1]], norm_all.at[x, m], target, hid_x_first + o))
    norm_all[x, m] = norm_out[x]

    def make_gather(block, halves, first):
        came = {o: lax.rem(m - 2 * o + NM, NM) for o in range(NY)}
        along = {o: remote(block(m), block(m), at_y(o), first + i) for i, o in enumerate((1, 3))}
        onward = {
            o: remote(halves(came[o])[i], halves(came[o])[i], at_y(o), first + 2 + i)
            for i, o in enumerate((1, 3))
        }
        across = {
            o: remote(block(came[o]), block(came[o]), sibling, first + 4 + o) for o in range(NY)
        }
        return along, onward, across

    def gather_start(gather):
        along, onward, across = gather
        start(along[1])
        start(along[3])
        start(across[0])

    def gather_pass(gather):
        along, onward, across = gather
        for o in (1, 3):
            along[o].wait_recv()
            start(onward[o])
            start(across[o])

    def gather_last(gather):
        along, onward, across = gather
        for o in (1, 3):
            onward[o].wait_recv()
        start(across[2])

    lat_gather = make_gather(
        lambda who: lat_all.at[who],
        lambda who: (lat_all.at[who, pl.ds(0, 4)], lat_all.at[who, pl.ds(4, 4)]),
        take(8),
    )
    hid_first = take(8 * NX)

    def hid_gather(k):
        return make_gather(
            lambda who: norm_all.at[k, who],
            lambda who: (norm_all.at[k, who, pl.ds(0, 16)], norm_all.at[k, who, pl.ds(16, 16)]),
            hid_first + 8 * k,
        )

    def hid_start(k):
        along, onward, across = hid_gather(k)
        for copy in (along[1], along[3], across[0]):
            copy.start()

    hid_start(x)

    lane_owner = lax.broadcasted_iota(jnp.int32, (1, 128), 1) // 16

    def positions(source_z, first):
        for source_x in range(NX):
            block = (source_z * NX + source_x) * 4
            slot_pos = [jnp.int32(FAR), jnp.int32(FAR)]
            seen = jnp.int32(0)
            for i in range(4):
                match = doc_ref[0, block + i] == z
                place = pos_ref[0, block + i]
                for r in range(2):
                    slot_pos[r] = jnp.where(match & (seen == r), place, slot_pos[r])
                seen = seen + jnp.where(match, 1, 0)
            for r in range(2):
                key_pos[source_x * 2 + r] = jnp.where(
                    lane_owner == source_z, slot_pos[r], key_pos[source_x * 2 + r]
                )
                first = jnp.minimum(first, slot_pos[r])
        return first

    key_pos[...] = jnp.full(key_pos.shape, FAR, jnp.int32)
    first_pos = lax.fori_loop(0, NZ, positions, jnp.int32(FAR))

    for copy in lat_z:
        copy.wait_recv()
    gather_start(lat_gather)
    ring_start(ring_q, 0)
    kv_sends = []

    def keys_values(o):
        chip = lax.rem(y - o + NY, NY)
        rows = lat_all[pl.ds(chip * 2, 2)].reshape(256, 1280)
        for weight, at in ((wk_v, 0), (wv_v, HEAD_DIM)):
            made = dot(rows, weight[...]).astype(BF16)
            for head in range(NX):
                kv_out[head, chip, :, at : at + HEAD_DIM] = made[
                    :, head * HEAD_DIM : (head + 1) * HEAD_DIM
                ]
        for off in (1, 3, 2):
            target = at_x(off)
            copy = remote(kv_out.at[target[1], chip], kv_all.at[x, chip], target)
            start(copy)
            kv_sends.append(copy)
        kv_all[x, chip] = kv_out[x, chip]

    loads[2].wait()
    loads[3].wait()
    lat_gather[2][0].wait_recv()
    keys_values(0)
    ring_start(ring_q, 1)
    gather_pass(lat_gather)
    for k in range(NX):

        @pl.when(x != k)
        def _():
            off = lax.rem(x - k + NX, NX)
            remote(norm_out.at[k], norm_all.at[k, m], at_x(off), hid_x_first + off).wait_recv()
            hid_start(k)

    hid_gathers = [hid_gather(k) for k in range(NX)]
    for gather in hid_gathers:
        sent.extend((gather[0][1], gather[0][3], gather[2][0]))
    for o in (1, 3):
        lat_gather[2][o].wait_recv()
        keys_values(o)
    ring_start(ring_q, 2)
    gather_last(lat_gather)
    gather_pass(hid_gathers[0])
    lat_gather[2][2].wait_recv()
    keys_values(2)
    gather_pass(hid_gathers[1])
    gather_last(hid_gathers[0])
    ring_start(ring_q, 3)
    gather_pass(hid_gathers[2])
    gather_last(hid_gathers[1])

    ring_wait(ring_q, 3)
    ring_start(ring_o, 0)
    loads[4].wait()
    halves = {1: pl.ds(0, 128), 3: pl.ds(128, 128)}
    far = lax.rem(x + 2, NX)
    q_far, q_near = [], []
    for k in range(NX):
        q_far.append({
            o: remote(q_out.at[k, far, halves[o]], q_mid.at[k, halves[o]], at_x(o))
            for o in (1, 3)
        })
        q_near.append({
            o: remote(q_out.at[k, at_x(o)[1]], q_in.at[k, i], at_x(o))
            for i, o in enumerate((1, 3))
        })

    def send_near(k):
        for o in (1, 3):
            q_far[k][o].wait_recv()
            to = at_x(o)[1]
            q_out[k, to, halves[o]] = q_out[k, to, halves[o]] + q_mid[k, halves[o]]
            start(q_near[k][o])

    def ask(k):
        for o in range(NY):
            hid_gathers[k][2][o].wait_recv()
        made = dot(norm_all[k].reshape(256, 2048), wq_all[...].reshape(2048, 512))
        for head in range(NX):
            q_out[k, head] = made[:, head * HEAD_DIM : (head + 1) * HEAD_DIM]
        for o in (1, 3):
            start(q_far[k][o])

    ask(0)
    gather_pass(hid_gathers[3])
    gather_last(hid_gathers[2])
    ask(1)
    send_near(0)
    gather_last(hid_gathers[3])
    ring_start(ring_o, 1)
    ask(2)
    send_near(1)
    ask(3)

    for copy in kv_sends:
        copy.wait_recv()

    head_lanes = pl.ds(pl.multiple_of(x * HEAD_DIM, HEAD_DIM), HEAD_DIM)
    att_sends = {}

    def attend(k):
        for o in (1, 3):
            q_near[k][o].wait_recv()
        query = (q_out[k, x] + q_in[k, 0] + q_in[k, 1]).astype(BF16)
        text_pos = lax.broadcasted_iota(jnp.int32, (256, 128), 0) + k * 256

        def score(i, top):
            block = kv_all[i // 2, pl.ds(lax.rem(i, 2) * 2, 2)].reshape(512, 256)
            raw = lax.dot_general(
                query, block[:, :HEAD_DIM], (((1,), (1,)), ((), ())), preferred_element_type=F32
            )
            visible = key_pos[i] <= text_pos
            for g in range(4):
                part = jnp.where(visible, raw[:, g * 128 : (g + 1) * 128], MASKED)
                scores[i, :, g * 128 : (g + 1) * 128] = part
                top = jnp.maximum(top, part)
            return top

        top = lax.fori_loop(0, 8, score, jnp.full((256, 128), MASKED, F32), unroll=True)
        row_max = jnp.max(top, axis=-1, keepdims=True)

        def mix(i, carry):
            mixed, running = carry
            weights = jnp.exp2((scores[i] - row_max) * (HEAD_DIM ** (-0.5) * LOG2E))
            for g in range(4):
                running = running + weights[:, g * 128 : (g + 1) * 128]
            block = kv_all[i // 2, pl.ds(lax.rem(i, 2) * 2, 2)].reshape(512, 256)
            return mixed + dot(weights.astype(BF16), block[:, HEAD_DIM:]), running

        zero = jnp.zeros((256, 128), F32)
        mixed, running = lax.fori_loop(0, 8, mix, (zero, zero), unroll=True)
        att_all[k, :, head_lanes] = (
            mixed / jnp.sum(running, axis=-1, keepdims=True)
        ).astype(BF16)
        copies = []
        for off in (1, 3, 2):
            copy = remote(att_all.at[k, :, head_lanes], att_all.at[k, :, head_lanes], at_x(off))
            start(copy)
            copies.append(copy)
        att_sends[k] = copies

    y_far = lax.rem(y + 2, NY)
    pairs, sum_far, sum_near = {}, {}, {}

    def chip_sum(k, to):
        return pair_own[k, to].astype(F32) + pair_in[k, to].astype(F32)

    def project(k):
        for copy in att_sends[k]:
            copy.wait_recv()
        rows = att_all[k]

        def other(i, carry):
            pair_out[k, i] = dot(rows, wo_all[2 * i + 1 - c]).astype(BF16)
            return carry

        lax.fori_loop(0, NY, other, 0, unroll=True)
        pairs[k] = remote(pair_out.at[k], pair_in.at[k], sibling)
        start(pairs[k])

        def mine(i, carry):
            pair_own[k, i] = dot(rows, wo_all[2 * i + c]).astype(BF16)
            return carry

        lax.fori_loop(0, NY, mine, 0, unroll=True)

    def send_sum(k):
        pairs[k].wait_recv()
        sum_out[k, y_far] = chip_sum(k, y_far).astype(BF16)
        sum_far[k] = {}
        for o in (1, 3):
            sum_far[k][o] = remote(
                sum_out.at[k, y_far, halves[o]], sum_mid.at[k, halves[o]], at_y(o)
            )
            start(sum_far[k][o])

    def pass_sum(k):
        sum_near[k] = {}
        for i, o in enumerate((1, 3)):
            to = lax.rem(y + o, NY)
            total = chip_sum(k, to)
            sum_far[k][o].wait_recv()
            passed = sum_mid[k, halves[o]].astype(F32)
            at = 0 if o == 1 else 128
            sum_out[k, to, halves[o]] = (total[at : at + 128] + passed).astype(BF16)
            rest = 128 - at
            sum_out[k, to, halves[4 - o]] = total[rest : rest + 128].astype(BF16)
            sum_near[k][o] = remote(sum_out.at[k, to], sum_in.at[k, i], at_y(o))
            start(sum_near[k][o])

    out_cols = pl.ds(pl.multiple_of(x * 256, 256), 256)
    gate_here = jnp.tanh(gate[:, out_cols])
    fin_sends = []
    first_fin = take(NX * 2)

    def finish(k):
        for o in (1, 3):
            sum_near[k][o].wait_recv()
        total = chip_sum(k, y) + sum_in[k, 0].astype(F32) + sum_in[k, 1].astype(F32)
        present = lax.broadcasted_iota(jnp.int32, (256, 256), 0) + k * 256 >= first_pos
        result = total * gate_here * jnp.where(present, 1.0, 0.0)
        fin_out[k] = result.astype(BF16)
        copy = pltpu.make_async_remote_copy(
            src_ref=fin_out.at[k], dst_ref=out.at[0, :, out_cols],
            send_sem=send_sems.at[first_fin + k], recv_sem=recv_sems.at[first_fin + NX + x],
            device_id=(z, k, m), device_id_type=pl.DeviceIdType.MESH,
        )
        keep = pltpu.make_async_copy(fin_out.at[k], out.at[0, :, out_cols], local_sems.at[6])

        @pl.when(x == k)
        def _():
            keep.start()

        @pl.when(x != k)
        def _():
            copy.start()

        fin_sends.append((copy, keep))

    attend(0)
    send_near(2)
    ring_start(ring_o, 2)
    attend(1)
    send_near(3)
    ring_start(ring_o, 3)
    ring_wait(ring_o, 3)
    loads[5].wait()
    project(0)
    attend(2)
    send_sum(0)
    project(1)
    attend(3)
    pass_sum(0)
    send_sum(1)
    project(2)
    pass_sum(1)
    finish(0)
    send_sum(2)
    project(3)
    pass_sum(2)
    finish(1)
    send_sum(3)
    finish(2)
    pass_sum(3)
    finish(3)

    for off in (1, 3, 2):
        source = lax.rem(x - off + NX, NX)
        cols = pl.ds(pl.multiple_of(source * 256, 256), 256)
        pltpu.make_async_remote_copy(
            src_ref=fin_out.at[0], dst_ref=out.at[0, :, cols],
            send_sem=send_sems.at[first_fin], recv_sem=recv_sems.at[first_fin + NX + source],
            device_id=at_x(off), device_id_type=pl.DeviceIdType.MESH,
        ).wait_recv()
    for k, (copy, keep) in enumerate(fin_sends):

        @pl.when(x == k)
        def _():
            keep.wait()

        @pl.when(x != k)
        def _():
            copy.wait_send()

    for copy in sent:
        copy.wait_send()


def on_device(
    hidden, norm_gain, w_query, w_key, w_value, w_out, gate_alpha, latents, image_doc, image_pos
):
    vmem = pl.BlockSpec(memory_space=pltpu.VMEM)
    smem = pl.BlockSpec(memory_space=pltpu.SMEM)
    anywhere = pl.BlockSpec(memory_space=pl.ANY)
    buffer = pltpu.VMEM
    return pl.pallas_call(
        kernel,
        out_shape=jax.ShapeDtypeStruct((1, 256, 1024), BF16),
        in_specs=[
            anywhere, vmem, anywhere, anywhere, anywhere, anywhere, vmem, anywhere, smem, smem,
        ],
        out_specs=anywhere,
        scratch_shapes=[
            buffer((32, 8192), BF16),
            buffer((4, 16, 1280), BF16),
            buffer((1280, 512), BF16),
            buffer((1280, 512), BF16),
            buffer((NZ, 16, 1280), BF16),
            buffer((NM, NZ, 16, 1280), BF16),
            buffer((NX, 32, 2048), BF16),
            buffer((NX, NM, 32, 2048), BF16),
            buffer((NZ, 256, 512), BF16),
            buffer((NZ, 512, 256), BF16),
            buffer((NX, NY, 256, 256), BF16),
            buffer((NX, NY, 256, 256), BF16),
            buffer((NX * 2, 1, 128), jnp.int32),
            buffer((NX, NX, 256, 128), F32),
            buffer((NX, 256, 128), F32),
            buffer((NX, 2, 256, 128), F32),
            buffer((8, 256, 512), F32),
            buffer((NX, 256, 512), BF16),
            buffer((NX, NY, 256, 256), BF16),
            buffer((NX, NY, 256, 256), BF16),
            buffer((NX, NY, 256, 256), BF16),
            buffer((NX, NY, 256, 256), BF16),
            buffer((NX, 256, 256), BF16),
            buffer((NX, 2, 256, 256), BF16),
            buffer((NX, 256, 256), BF16),
            pltpu.SemaphoreType.DMA((160,)),
            pltpu.SemaphoreType.DMA((160,)),
            pltpu.SemaphoreType.DMA((8,)),
        ],
        compiler_params=pltpu.CompilerParams(
            collective_id=0, has_side_effects=True, vmem_limit_bytes=56 * 2**20
        ),
    )(
        hidden, norm_gain.reshape(1, -1), w_query, w_key, w_value, w_out,
        gate_alpha.reshape(1, -1), latents, image_doc.reshape(1, -1), image_pos.reshape(1, -1),
    )


def solution(mesh):
    placed = (
        P("dp", "seq", None),
        P(),
        P(("dp", "seq"), "mp"),
        P(None, "mp"),
        P(None, "mp"),
        P("mp", ("dp", "seq")),
        P("mp"),
        P(("dp", "seq"), None, None),
        P(),
        P(),
    )
    return jax.shard_map(
        on_device, mesh=mesh, in_specs=placed, out_specs=P("dp", "seq", "mp"), check_vma=False
    )
```

```python
import functools

import jax
import jax.numpy as jnp
from jax import lax
from jax.experimental import pallas as pl
from jax.experimental.pallas import tpu as pltpu
from jax.sharding import PartitionSpec as P

HEAD_DIM = 128
EPSILON = 1e-05
NZ, NX, NM, NY = 8, 4, 8, 4
LOG2E = 1.4426950408889634
MASKED = -1e30
FAR = 1 << 20
BF16, F32 = jnp.bfloat16, jnp.float32


def dot(a, b):
    return jnp.dot(a, b, preferred_element_type=F32)


def kernel(
    hidden, gain, w_query, w_key, w_value, w_out, gate, latents, doc_ref, pos_ref,
    out,
    hid_v, lat_v, wk_v, wv_v, lat_out, lat_all, norm_out, norm_all, wq_all, wo_all,
    kv_out, kv_all, key_pos, q_out, q_mid, q_in, scores, att_all,
    pair_out, pair_own, pair_in, sum_out, sum_mid, sum_in, fin_out,
    send_sems, recv_sems, local_sems,
):
    z, x, m = lax.axis_index("dp"), lax.axis_index("seq"), lax.axis_index("mp")
    y, c = m // 2, lax.rem(m, 2)
    sibling = (z, x, m + 1 - 2 * c)

    def at_z(off):
        return (lax.rem(z + off + NZ, NZ), x, m)

    def at_x(off):
        return (z, lax.rem(x + off, NX), m)

    def at_y(off):
        return (z, x, lax.rem(m + 2 * off, NM))

    taken = [0]
    sent = []

    def take(count):
        first = taken[0]
        taken[0] += count
        return first

    def remote(src, dst, device, slot=None):
        if slot is None:
            slot = take(1)
        return pltpu.make_async_remote_copy(
            src_ref=src, dst_ref=dst, send_sem=send_sems.at[slot], recv_sem=recv_sems.at[slot],
            device_id=device, device_id_type=pl.DeviceIdType.MESH,
        )

    def start(copy):
        copy.start()
        sent.append(copy)

    partners = [at_z(o) for o in range(1, NZ)] + [at_x(o) for o in range(1, NX)]
    partners += [at_y(o) for o in range(1, NY)] + [sibling]
    barrier = pltpu.get_barrier_semaphore()
    for partner in partners:
        pl.semaphore_signal(
            barrier, inc=1, device_id=partner, device_id_type=pl.DeviceIdType.MESH
        )

    tok_part = pl.ds(pl.multiple_of(m * 32, 32), 32)
    lat_part = pl.ds(pl.multiple_of(lax.rem(m, 4) * 16, 16), 16)
    loads = [
        pltpu.make_async_copy(s, d, local_sems.at[i])
        for i, (s, d) in enumerate((
            (latents.at[:, lat_part, :], lat_v),
            (hidden.at[0, tok_part, :], hid_v),
            (w_key, wk_v),
            (w_value, wv_v),
            (w_query, wq_all.at[z]),
            (w_out, wo_all.at[z]),
        ))
    ]
    for load in loads:
        load.start()

    def make_ring(own, buf):
        half = own.shape[0] // 2
        steps = []
        for s in range(4):
            up_from, down_from = lax.rem(z - s + NZ, NZ), lax.rem(z + s, NZ)
            up, down = buf.at[up_from], buf.at[down_from]
            if s == 3:
                up, down = buf.at[up_from, pl.ds(0, half)], buf.at[down_from, pl.ds(half, half)]
            steps.append((
                remote(own if s == 0 else up, up, at_z(1)),
                remote(own if s == 0 else down, down, at_z(-1)),
            ))
        return steps

    ring_q = make_ring(w_query, wq_all)
    ring_o = make_ring(w_out, wo_all)

    def ring_start(ring, s):
        if s > 0:
            ring_wait(ring, s - 1)
        for copy in ring[s]:
            start(copy)

    def ring_wait(ring, s):
        for copy in ring[s]:
            copy.wait_recv()

    base = (z * NX + x) * 4
    docs = [doc_ref[0, base + i] for i in range(4)]
    ranks = []
    for i in range(4):
        rank = jnp.int32(0)
        for before in range(i):
            rank = rank + jnp.where(docs[before] == docs[i], 1, 0)
        ranks.append(rank)
    slot_here = m // 4
    loads[0].wait()

    def route(doc, carry):
        total = None
        for i in range(4):
            chosen = (docs[i] == doc) & (ranks[i] == slot_here)
            term = lat_v[i].astype(F32) * jnp.where(chosen, 1.0, 0.0).astype(F32)
            total = term if total is None else total + term
        lat_out[doc] = total.astype(BF16)
        return carry

    lax.fori_loop(0, NZ, route, 0)
    pl.semaphore_wait(barrier, len(partners))
    lat_z = []
    for o in range(1, NZ):
        target = at_z(o)
        copy = remote(lat_out.at[target[0]], lat_all.at[m, z], target)
        start(copy)
        lat_z.append(copy)
    lat_all[m, z] = lat_out[z]

    loads[1].wait()

    def square_sum(i, total):
        part = hid_v[:, pl.ds(pl.multiple_of(i * 1024, 1024), 1024)].astype(F32)
        return total + jnp.sum(part * part, axis=-1, keepdims=True)

    mean_square = lax.fori_loop(0, 8, square_sum, jnp.zeros((32, 1), F32)) / 8192.0
    inverse = lax.rsqrt(mean_square + EPSILON)

    def normalise(i, carry):
        cols = pl.ds(pl.multiple_of(i * 1024, 1024), 1024)
        rows = (hid_v[:, cols].astype(F32) * inverse * gain[:, cols]).astype(BF16)
        for owner in range(NX):
            norm_out[owner, :, pl.ds(pl.multiple_of(i * 256, 256), 256)] = rows[
                :, owner * 256 : owner * 256 + 256
            ]
        return carry

    lax.fori_loop(0, 8, normalise, 0)
    hid_x_first = take(NX)
    for o in (1, 3, 2):
        target = at_x(o)
        start(remote(norm_out.at[target[1]], norm_all.at[x, m], target, hid_x_first + o))
    norm_all[x, m] = norm_out[x]

    def make_gather(block, halves, first):
        came = {o: lax.rem(m - 2 * o + NM, NM) for o in range(NY)}
        along = {o: remote(block(m), block(m), at_y(o), first + i) for i, o in enumerate((1, 3))}
        onward = {
            o: remote(halves(came[o])[i], halves(came[o])[i], at_y(o), first + 2 + i)
            for i, o in enumerate((1, 3))
        }
        across = {
            o: remote(block(came[o]), block(came[o]), sibling, first + 4 + o) for o in range(NY)
        }
        return along, onward, across

    def gather_start(gather):
        along, onward, across = gather
        start(along[1])
        start(along[3])
        start(across[0])

    def gather_pass(gather):
        along, onward, across = gather
        for o in (1, 3):
            along[o].wait_recv()
            start(onward[o])
            start(across[o])

    def gather_last(gather):
        along, onward, across = gather
        for o in (1, 3):
            onward[o].wait_recv()
        start(across[2])

    lat_gather = make_gather(
        lambda who: lat_all.at[who],
        lambda who: (lat_all.at[who, pl.ds(0, 4)], lat_all.at[who, pl.ds(4, 4)]),
        take(8),
    )
    hid_first = take(8 * NX)

    def hid_gather(k):
        return make_gather(
            lambda who: norm_all.at[k, who],
            lambda who: (norm_all.at[k, who, pl.ds(0, 16)], norm_all.at[k, who, pl.ds(16, 16)]),
            hid_first + 8 * k,
        )

    def hid_start(k):
        along, onward, across = hid_gather(k)
        for copy in (along[1], along[3], across[0]):
            copy.start()

    hid_start(x)
    ring_start(ring_q, 0)

    lane_owner = lax.broadcasted_iota(jnp.int32, (1, 128), 1) // 16

    def positions(source_z, first):
        for source_x in range(NX):
            block = (source_z * NX + source_x) * 4
            slot_pos = [jnp.int32(FAR), jnp.int32(FAR)]
            seen = jnp.int32(0)
            for i in range(4):
                match = doc_ref[0, block + i] == z
                place = pos_ref[0, block + i]
                for r in range(2):
                    slot_pos[r] = jnp.where(match & (seen == r), place, slot_pos[r])
                seen = seen + jnp.where(match, 1, 0)
            for r in range(2):
                key_pos[source_x * 2 + r] = jnp.where(
                    lane_owner == source_z, slot_pos[r], key_pos[source_x * 2 + r]
                )
                first = jnp.minimum(first, slot_pos[r])
        return first

    key_pos[...] = jnp.full(key_pos.shape, FAR, jnp.int32)
    first_pos = lax.fori_loop(0, NZ, positions, jnp.int32(FAR))

    for copy in lat_z:
        copy.wait_recv()
    gather_start(lat_gather)
    kv_sends = []

    def keys_values(o):
        chip = lax.rem(y - o + NY, NY)
        rows = lat_all[pl.ds(chip * 2, 2)].reshape(256, 1280)
        for weight, at in ((wk_v, 0), (wv_v, HEAD_DIM)):
            made = dot(rows, weight[...]).astype(BF16)
            for head in range(NX):
                kv_out[head, chip, :, at : at + HEAD_DIM] = made[
                    :, head * HEAD_DIM : (head + 1) * HEAD_DIM
                ]
        for off in (1, 3, 2):
            target = at_x(off)
            copy = remote(kv_out.at[target[1], chip], kv_all.at[x, chip], target)
            start(copy)
            kv_sends.append(copy)
        kv_all[x, chip] = kv_out[x, chip]

    loads[2].wait()
    loads[3].wait()
    lat_gather[2][0].wait_recv()
    keys_values(0)
    ring_start(ring_q, 1)
    gather_pass(lat_gather)
    for k in range(NX):

        @pl.when(x != k)
        def _():
            off = lax.rem(x - k + NX, NX)
            remote(norm_out.at[k], norm_all.at[k, m], at_x(off), hid_x_first + off).wait_recv()
            hid_start(k)

    hid_gathers = [hid_gather(k) for k in range(NX)]
    for gather in hid_gathers:
        sent.extend((gather[0][1], gather[0][3], gather[2][0]))
    for o in (1, 3):
        lat_gather[2][o].wait_recv()
        keys_values(o)
    ring_start(ring_q, 2)
    gather_last(lat_gather)
    gather_pass(hid_gathers[0])
    lat_gather[2][2].wait_recv()
    keys_values(2)
    gather_pass(hid_gathers[1])
    gather_last(hid_gathers[0])
    ring_start(ring_q, 3)
    ring_start(ring_o, 0)
    gather_pass(hid_gathers[2])
    gather_last(hid_gathers[1])

    ring_wait(ring_q, 3)
    loads[4].wait()
    halves = {1: pl.ds(0, 128), 3: pl.ds(128, 128)}
    far = lax.rem(x + 2, NX)
    q_far, q_near = [], []
    for k in range(NX):
        q_far.append({
            o: remote(q_out.at[k, far, halves[o]], q_mid.at[k, halves[o]], at_x(o))
            for o in (1, 3)
        })
        q_near.append({
            o: remote(q_out.at[k, at_x(o)[1]], q_in.at[k, i], at_x(o))
            for i, o in enumerate((1, 3))
        })

    def send_near(k):
        for o in (1, 3):
            q_far[k][o].wait_recv()
            to = at_x(o)[1]
            q_out[k, to, halves[o]] = q_out[k, to, halves[o]] + q_mid[k, halves[o]]
            start(q_near[k][o])

    def ask(k):
        for o in range(NY):
            hid_gathers[k][2][o].wait_recv()
        made = dot(norm_all[k].reshape(256, 2048), wq_all[...].reshape(2048, 512))
        for head in range(NX):
            q_out[k, head] = made[:, head * HEAD_DIM : (head + 1) * HEAD_DIM]
        for o in (1, 3):
            start(q_far[k][o])

    ask(0)
    gather_pass(hid_gathers[3])
    gather_last(hid_gathers[2])
    ask(1)
    send_near(0)
    gather_last(hid_gathers[3])
    ring_start(ring_o, 1)
    ask(2)
    send_near(1)
    ask(3)

    ring_start(ring_o, 2)
    for copy in kv_sends:
        copy.wait_recv()

    head_lanes = pl.ds(pl.multiple_of(x * HEAD_DIM, HEAD_DIM), HEAD_DIM)
    att_sends = {}

    def attend(k):
        for o in (1, 3):
            q_near[k][o].wait_recv()
        query = (q_out[k, x] + q_in[k, 0] + q_in[k, 1]).astype(BF16)
        text_pos = lax.broadcasted_iota(jnp.int32, (256, 128), 0) + k * 256

        def score(i, top):
            block = kv_all[i // 2, pl.ds(lax.rem(i, 2) * 2, 2)].reshape(512, 256)
            raw = lax.dot_general(
                query, block[:, :HEAD_DIM], (((1,), (1,)), ((), ())), preferred_element_type=F32
            )
            visible = key_pos[i] <= text_pos
            for g in range(4):
                part = jnp.where(visible, raw[:, g * 128 : (g + 1) * 128], MASKED)
                scores[i, :, g * 128 : (g + 1) * 128] = part
                top = jnp.maximum(top, part)
            return top

        top = lax.fori_loop(0, 8, score, jnp.full((256, 128), MASKED, F32), unroll=True)
        row_max = jnp.max(top, axis=-1, keepdims=True)

        def mix(i, carry):
            mixed, running = carry
            weights = jnp.exp2((scores[i] - row_max) * (HEAD_DIM ** (-0.5) * LOG2E))
            for g in range(4):
                running = running + weights[:, g * 128 : (g + 1) * 128]
            block = kv_all[i // 2, pl.ds(lax.rem(i, 2) * 2, 2)].reshape(512, 256)
            return mixed + dot(weights.astype(BF16), block[:, HEAD_DIM:]), running

        zero = jnp.zeros((256, 128), F32)
        mixed, running = lax.fori_loop(0, 8, mix, (zero, zero), unroll=True)
        att_all[k, :, head_lanes] = (
            mixed / jnp.sum(running, axis=-1, keepdims=True)
        ).astype(BF16)
        copies = []
        for off in (1, 3, 2):
            copy = remote(att_all.at[k, :, head_lanes], att_all.at[k, :, head_lanes], at_x(off))
            start(copy)
            copies.append(copy)
        att_sends[k] = copies

    y_far = lax.rem(y + 2, NY)
    pairs, sum_far, sum_near = {}, {}, {}

    def chip_sum(k, to):
        return pair_own[k, to].astype(F32) + pair_in[k, to].astype(F32)

    def project(k):
        for copy in att_sends[k]:
            copy.wait_recv()
        rows = att_all[k]

        def other(i, carry):
            pair_out[k, i] = dot(rows, wo_all[2 * i + 1 - c]).astype(BF16)
            return carry

        lax.fori_loop(0, NY, other, 0, unroll=True)
        pairs[k] = remote(pair_out.at[k], pair_in.at[k], sibling)
        start(pairs[k])

        def mine(i, carry):
            pair_own[k, i] = dot(rows, wo_all[2 * i + c]).astype(BF16)
            return carry

        lax.fori_loop(0, NY, mine, 0, unroll=True)

    def send_sum(k):
        pairs[k].wait_recv()
        sum_out[k, y_far] = chip_sum(k, y_far).astype(BF16)
        sum_far[k] = {}
        for o in (1, 3):
            sum_far[k][o] = remote(
                sum_out.at[k, y_far, halves[o]], sum_mid.at[k, halves[o]], at_y(o)
            )
            start(sum_far[k][o])

    def pass_sum(k):
        sum_near[k] = {}
        for i, o in enumerate((1, 3)):
            to = lax.rem(y + o, NY)
            total = chip_sum(k, to)
            sum_far[k][o].wait_recv()
            passed = sum_mid[k, halves[o]].astype(F32)
            at = 0 if o == 1 else 128
            sum_out[k, to, halves[o]] = (total[at : at + 128] + passed).astype(BF16)
            rest = 128 - at
            sum_out[k, to, halves[4 - o]] = total[rest : rest + 128].astype(BF16)
            sum_near[k][o] = remote(sum_out.at[k, to], sum_in.at[k, i], at_y(o))
            start(sum_near[k][o])

    out_cols = pl.ds(pl.multiple_of(x * 256, 256), 256)
    gate_here = jnp.tanh(gate[:, out_cols])
    fin_sends = []
    first_fin = take(NX * 2)

    def finish(k):
        for o in (1, 3):
            sum_near[k][o].wait_recv()
        total = chip_sum(k, y) + sum_in[k, 0].astype(F32) + sum_in[k, 1].astype(F32)
        present = lax.broadcasted_iota(jnp.int32, (256, 256), 0) + k * 256 >= first_pos
        result = total * gate_here * jnp.where(present, 1.0, 0.0)
        fin_out[k] = result.astype(BF16)
        copy = pltpu.make_async_remote_copy(
            src_ref=fin_out.at[k], dst_ref=out.at[0, :, out_cols],
            send_sem=send_sems.at[first_fin + k], recv_sem=recv_sems.at[first_fin + NX + x],
            device_id=(z, k, m), device_id_type=pl.DeviceIdType.MESH,
        )
        keep = pltpu.make_async_copy(fin_out.at[k], out.at[0, :, out_cols], local_sems.at[6])

        @pl.when(x == k)
        def _():
            keep.start()

        @pl.when(x != k)
        def _():
            copy.start()

        fin_sends.append((copy, keep))

    attend(0)
    send_near(2)
    ring_start(ring_o, 3)
    send_near(3)
    attend(1)
    attend(2)
    ring_wait(ring_o, 3)
    loads[5].wait()
    project(0)
    project(1)
    send_sum(0)
    attend(3)
    send_sum(1)
    pass_sum(0)
    project(2)
    pass_sum(1)
    send_sum(2)
    project(3)
    finish(0)
    send_sum(3)
    pass_sum(2)
    finish(1)
    pass_sum(3)
    finish(2)
    finish(3)

    for off in (1, 3, 2):
        source = lax.rem(x - off + NX, NX)
        cols = pl.ds(pl.multiple_of(source * 256, 256), 256)
        pltpu.make_async_remote_copy(
            src_ref=fin_out.at[0], dst_ref=out.at[0, :, cols],
            send_sem=send_sems.at[first_fin], recv_sem=recv_sems.at[first_fin + NX + source],
            device_id=at_x(off), device_id_type=pl.DeviceIdType.MESH,
        ).wait_recv()
    for k, (copy, keep) in enumerate(fin_sends):

        @pl.when(x == k)
        def _():
            keep.wait()

        @pl.when(x != k)
        def _():
            copy.wait_send()

    for copy in sent:
        copy.wait_send()


def on_device(
    hidden, norm_gain, w_query, w_key, w_value, w_out, gate_alpha, latents, image_doc, image_pos
):
    vmem = pl.BlockSpec(memory_space=pltpu.VMEM)
    smem = pl.BlockSpec(memory_space=pltpu.SMEM)
    anywhere = pl.BlockSpec(memory_space=pl.ANY)
    buffer = pltpu.VMEM
    return pl.pallas_call(
        kernel,
        out_shape=jax.ShapeDtypeStruct((1, 256, 1024), BF16),
        in_specs=[
            anywhere, vmem, anywhere, anywhere, anywhere, anywhere, vmem, anywhere, smem, smem,
        ],
        out_specs=anywhere,
        scratch_shapes=[
            buffer((32, 8192), BF16),
            buffer((4, 16, 1280), BF16),
            buffer((1280, 512), BF16),
            buffer((1280, 512), BF16),
            buffer((NZ, 16, 1280), BF16),
            buffer((NM, NZ, 16, 1280), BF16),
            buffer((NX, 32, 2048), BF16),
            buffer((NX, NM, 32, 2048), BF16),
            buffer((NZ, 256, 512), BF16),
            buffer((NZ, 512, 256), BF16),
            buffer((NX, NY, 256, 256), BF16),
            buffer((NX, NY, 256, 256), BF16),
            buffer((NX * 2, 1, 128), jnp.int32),
            buffer((NX, NX, 256, 128), F32),
            buffer((NX, 256, 128), F32),
            buffer((NX, 2, 256, 128), F32),
            buffer((8, 256, 512), F32),
            buffer((NX, 256, 512), BF16),
            buffer((NX, NY, 256, 256), BF16),
            buffer((NX, NY, 256, 256), BF16),
            buffer((NX, NY, 256, 256), BF16),
            buffer((NX, NY, 256, 256), BF16),
            buffer((NX, 256, 256), BF16),
            buffer((NX, 2, 256, 256), BF16),
            buffer((NX, 256, 256), BF16),
            pltpu.SemaphoreType.DMA((160,)),
            pltpu.SemaphoreType.DMA((160,)),
            pltpu.SemaphoreType.DMA((8,)),
        ],
        compiler_params=pltpu.CompilerParams(
            collective_id=0, has_side_effects=True, vmem_limit_bytes=56 * 2**20
        ),
    )(
        hidden, norm_gain.reshape(1, -1), w_query, w_key, w_value, w_out,
        gate_alpha.reshape(1, -1), latents, image_doc.reshape(1, -1), image_pos.reshape(1, -1),
    )


def solution(mesh):
    placed = (
        P("dp", "seq", None),
        P(),
        P(("dp", "seq"), "mp"),
        P(None, "mp"),
        P(None, "mp"),
        P("mp", ("dp", "seq")),
        P("mp"),
        P(("dp", "seq"), None, None),
        P(),
        P(),
    )
    return jax.shard_map(
        on_device, mesh=mesh, in_specs=placed, out_specs=P("dp", "seq", "mp"), check_vma=False
    )
```

```python
import functools

import jax
import jax.numpy as jnp
from jax import lax
from jax.experimental import pallas as pl
from jax.experimental.pallas import tpu as pltpu
from jax.sharding import PartitionSpec as P

HEAD_DIM = 128
EPSILON = 1e-05
NZ, NX, NM, NY = 8, 4, 8, 4
LOG2E = 1.4426950408889634
MASKED = -1e30
FAR = 1 << 20
BF16, F32 = jnp.bfloat16, jnp.float32


def dot(a, b):
    return jnp.dot(a, b, preferred_element_type=F32)


def kernel(
    hidden, gain, w_query, w_key, w_value, w_out, gate, latents, doc_ref, pos_ref,
    out,
    hid_v, lat_v, wk_v, wv_v, lat_out, lat_all, norm_out, norm_all, wq_all, wo_all,
    kv_out, kv_all, key_pos, q_out, q_mid, q_in, scores, att_all,
    pair_out, pair_own, pair_in, sum_out, sum_mid, sum_in, fin_out,
    send_sems, recv_sems, local_sems,
):
    z, x, m = lax.axis_index("dp"), lax.axis_index("seq"), lax.axis_index("mp")
    y, c = m // 2, lax.rem(m, 2)
    sibling = (z, x, m + 1 - 2 * c)

    def at_z(off):
        return (lax.rem(z + off + NZ, NZ), x, m)

    def at_x(off):
        return (z, lax.rem(x + off, NX), m)

    def at_y(off):
        return (z, x, lax.rem(m + 2 * off, NM))

    taken = [0]
    sent = []

    def take(count):
        first = taken[0]
        taken[0] += count
        return first

    def remote(src, dst, device, slot=None):
        if slot is None:
            slot = take(1)
        return pltpu.make_async_remote_copy(
            src_ref=src, dst_ref=dst, send_sem=send_sems.at[slot], recv_sem=recv_sems.at[slot],
            device_id=device, device_id_type=pl.DeviceIdType.MESH,
        )

    def start(copy):
        copy.start()
        sent.append(copy)

    partners = [at_z(o) for o in range(1, NZ)] + [at_x(o) for o in range(1, NX)]
    partners += [at_y(o) for o in range(1, NY)] + [sibling]
    barrier = pltpu.get_barrier_semaphore()
    for partner in partners:
        pl.semaphore_signal(
            barrier, inc=1, device_id=partner, device_id_type=pl.DeviceIdType.MESH
        )

    tok_part = pl.ds(pl.multiple_of(m * 32, 32), 32)
    lat_part = pl.ds(pl.multiple_of(lax.rem(m, 4) * 16, 16), 16)
    loads = [
        pltpu.make_async_copy(s, d, local_sems.at[i])
        for i, (s, d) in enumerate((
            (latents.at[:, lat_part, :], lat_v),
            (hidden.at[0, tok_part, :], hid_v),
            (w_key, wk_v),
            (w_value, wv_v),
            (w_query, wq_all.at[z]),
            (w_out, wo_all.at[z]),
        ))
    ]
    for load in loads:
        load.start()

    def make_ring(own, buf):
        half = own.shape[0] // 2
        steps = []
        for s in range(4):
            up_from, down_from = lax.rem(z - s + NZ, NZ), lax.rem(z + s, NZ)
            up, down = buf.at[up_from], buf.at[down_from]
            if s == 3:
                up, down = buf.at[up_from, pl.ds(0, half)], buf.at[down_from, pl.ds(half, half)]
            steps.append((
                remote(own if s == 0 else up, up, at_z(1)),
                remote(own if s == 0 else down, down, at_z(-1)),
            ))
        return steps

    ring_q = make_ring(w_query, wq_all)
    ring_o = make_ring(w_out, wo_all)

    def ring_start(ring, s):
        if s > 0:
            ring_wait(ring, s - 1)
        for copy in ring[s]:
            start(copy)

    def ring_wait(ring, s):
        for copy in ring[s]:
            copy.wait_recv()

    base = (z * NX + x) * 4
    docs = [doc_ref[0, base + i] for i in range(4)]
    ranks = []
    for i in range(4):
        rank = jnp.int32(0)
        for before in range(i):
            rank = rank + jnp.where(docs[before] == docs[i], 1, 0)
        ranks.append(rank)
    slot_here = m // 4
    loads[0].wait()

    def route(doc, carry):
        total = None
        for i in range(4):
            chosen = (docs[i] == doc) & (ranks[i] == slot_here)
            term = lat_v[i].astype(F32) * jnp.where(chosen, 1.0, 0.0).astype(F32)
            total = term if total is None else total + term
        lat_out[doc] = total.astype(BF16)
        return carry

    lax.fori_loop(0, NZ, route, 0)
    pl.semaphore_wait(barrier, len(partners))
    lat_z = []
    for o in range(1, NZ):
        target = at_z(o)
        copy = remote(lat_out.at[target[0]], lat_all.at[m, z], target)
        start(copy)
        lat_z.append(copy)
    lat_all[m, z] = lat_out[z]

    loads[1].wait()

    def square_sum(i, total):
        part = hid_v[:, pl.ds(pl.multiple_of(i * 1024, 1024), 1024)].astype(F32)
        return total + jnp.sum(part * part, axis=-1, keepdims=True)

    mean_square = lax.fori_loop(0, 8, square_sum, jnp.zeros((32, 1), F32)) / 8192.0
    inverse = lax.rsqrt(mean_square + EPSILON)

    def normalise(i, carry):
        cols = pl.ds(pl.multiple_of(i * 1024, 1024), 1024)
        rows = (hid_v[:, cols].astype(F32) * inverse * gain[:, cols]).astype(BF16)
        for owner in range(NX):
            norm_out[owner, :, pl.ds(pl.multiple_of(i * 256, 256), 256)] = rows[
                :, owner * 256 : owner * 256 + 256
            ]
        return carry

    lax.fori_loop(0, 8, normalise, 0)
    hid_x_first = take(NX)
    for o in (1, 3, 2):
        target = at_x(o)
        start(remote(norm_out.at[target[1]], norm_all.at[x, m], target, hid_x_first + o))
    norm_all[x, m] = norm_out[x]

    def make_gather(block, halves, first):
        came = {o: lax.rem(m - 2 * o + NM, NM) for o in range(NY)}
        along = {o: remote(block(m), block(m), at_y(o), first + i) for i, o in enumerate((1, 3))}
        onward = {
            o: remote(halves(came[o])[i], halves(came[o])[i], at_y(o), first + 2 + i)
            for i, o in enumerate((1, 3))
        }
        across = {
            o: remote(block(came[o]), block(came[o]), sibling, first + 4 + o) for o in range(NY)
        }
        return along, onward, across

    def gather_start(gather):
        along, onward, across = gather
        start(along[1])
        start(along[3])
        start(across[0])

    def gather_pass(gather):
        along, onward, across = gather
        for o in (1, 3):
            along[o].wait_recv()
            start(onward[o])
            start(across[o])

    def gather_last(gather):
        along, onward, across = gather
        for o in (1, 3):
            onward[o].wait_recv()
        start(across[2])

    lat_gather = make_gather(
        lambda who: lat_all.at[who],
        lambda who: (lat_all.at[who, pl.ds(0, 4)], lat_all.at[who, pl.ds(4, 4)]),
        take(8),
    )
    hid_first = take(8 * NX)

    def hid_gather(k):
        return make_gather(
            lambda who: norm_all.at[k, who],
            lambda who: (norm_all.at[k, who, pl.ds(0, 16)], norm_all.at[k, who, pl.ds(16, 16)]),
            hid_first + 8 * k,
        )

    def hid_start(k):
        along, onward, across = hid_gather(k)
        for copy in (along[1], along[3], across[0]):
            copy.start()

    hid_start(x)
    ring_start(ring_q, 0)

    lane_owner = lax.broadcasted_iota(jnp.int32, (1, 128), 1) // 16

    def positions(source_z, first):
        for source_x in range(NX):
            block = (source_z * NX + source_x) * 4
            slot_pos = [jnp.int32(FAR), jnp.int32(FAR)]
            seen = jnp.int32(0)
            for i in range(4):
                match = doc_ref[0, block + i] == z
                place = pos_ref[0, block + i]
                for r in range(2):
                    slot_pos[r] = jnp.where(match & (seen == r), place, slot_pos[r])
                seen = seen + jnp.where(match, 1, 0)
            for r in range(2):
                key_pos[source_x * 2 + r] = jnp.where(
                    lane_owner == source_z, slot_pos[r], key_pos[source_x * 2 + r]
                )
                first = jnp.minimum(first, slot_pos[r])
        return first

    key_pos[...] = jnp.full(key_pos.shape, FAR, jnp.int32)
    first_pos = lax.fori_loop(0, NZ, positions, jnp.int32(FAR))

    for copy in lat_z:
        copy.wait_recv()
    gather_start(lat_gather)
    kv_sends = []

    def keys_values(o):
        chip = lax.rem(y - o + NY, NY)
        rows = lat_all[pl.ds(chip * 2, 2)].reshape(256, 1280)
        for weight, at in ((wk_v, 0), (wv_v, HEAD_DIM)):
            made = dot(rows, weight[...]).astype(BF16)
            for head in range(NX):
                kv_out[head, chip, :, at : at + HEAD_DIM] = made[
                    :, head * HEAD_DIM : (head + 1) * HEAD_DIM
                ]
        for off in (1, 3, 2):
            target = at_x(off)
            copy = remote(kv_out.at[target[1], chip], kv_all.at[x, chip], target)
            start(copy)
            kv_sends.append(copy)
        kv_all[x, chip] = kv_out[x, chip]

    loads[2].wait()
    loads[3].wait()
    lat_gather[2][0].wait_recv()
    keys_values(0)
    ring_start(ring_q, 1)
    gather_pass(lat_gather)
    for k in range(NX):

        @pl.when(x != k)
        def _():
            off = lax.rem(x - k + NX, NX)
            remote(norm_out.at[k], norm_all.at[k, m], at_x(off), hid_x_first + off).wait_recv()
            hid_start(k)

    hid_gathers = [hid_gather(k) for k in range(NX)]
    for gather in hid_gathers:
        sent.extend((gather[0][1], gather[0][3], gather[2][0]))
    for o in (1, 3):
        lat_gather[2][o].wait_recv()
        keys_values(o)
    ring_start(ring_q, 2)
    ring_start(ring_o, 0)
    gather_last(lat_gather)
    gather_pass(hid_gathers[0])
    lat_gather[2][2].wait_recv()
    keys_values(2)
    gather_pass(hid_gathers[1])
    gather_last(hid_gathers[0])
    ring_start(ring_q, 3)
    gather_pass(hid_gathers[2])
    gather_last(hid_gathers[1])

    ring_wait(ring_q, 3)
    loads[4].wait()
    halves = {1: pl.ds(0, 128), 3: pl.ds(128, 128)}
    far = lax.rem(x + 2, NX)
    q_far, q_near = [], []
    for k in range(NX):
        q_far.append({
            o: remote(q_out.at[k, far, halves[o]], q_mid.at[k, halves[o]], at_x(o))
            for o in (1, 3)
        })
        q_near.append({
            o: remote(q_out.at[k, at_x(o)[1]], q_in.at[k, i], at_x(o))
            for i, o in enumerate((1, 3))
        })

    def send_near(k):
        for o in (1, 3):
            q_far[k][o].wait_recv()
            to = at_x(o)[1]
            q_out[k, to, halves[o]] = q_out[k, to, halves[o]] + q_mid[k, halves[o]]
            start(q_near[k][o])

    def ask(k):
        for o in range(NY):
            hid_gathers[k][2][o].wait_recv()
        made = dot(norm_all[k].reshape(256, 2048), wq_all[...].reshape(2048, 512))
        for head in range(NX):
            q_out[k, head] = made[:, head * HEAD_DIM : (head + 1) * HEAD_DIM]
        for o in (1, 3):
            start(q_far[k][o])

    ring_start(ring_o, 1)
    ask(0)
    gather_pass(hid_gathers[3])
    gather_last(hid_gathers[2])
    ask(1)
    send_near(0)
    gather_last(hid_gathers[3])
    ask(2)
    ring_start(ring_o, 2)
    send_near(1)
    ask(3)

    for copy in kv_sends:
        copy.wait_recv()

    head_lanes = pl.ds(pl.multiple_of(x * HEAD_DIM, HEAD_DIM), HEAD_DIM)
    att_sends = {}

    def attend(k):
        for o in (1, 3):
            q_near[k][o].wait_recv()
        query = (q_out[k, x] + q_in[k, 0] + q_in[k, 1]).astype(BF16)
        text_pos = lax.broadcasted_iota(jnp.int32, (256, 128), 0) + k * 256

        def score(i, top):
            block = kv_all[i // 2, pl.ds(lax.rem(i, 2) * 2, 2)].reshape(512, 256)
            raw = lax.dot_general(
                query, block[:, :HEAD_DIM], (((1,), (1,)), ((), ())), preferred_element_type=F32
            )
            visible = key_pos[i] <= text_pos
            for g in range(4):
                part = jnp.where(visible, raw[:, g * 128 : (g + 1) * 128], MASKED)
                scores[i, :, g * 128 : (g + 1) * 128] = part
                top = jnp.maximum(top, part)
            return top

        top = lax.fori_loop(0, 8, score, jnp.full((256, 128), MASKED, F32), unroll=True)
        row_max = jnp.max(top, axis=-1, keepdims=True)

        def mix(i, carry):
            mixed, running = carry
            weights = jnp.exp2((scores[i] - row_max) * (HEAD_DIM ** (-0.5) * LOG2E))
            for g in range(4):
                running = running + weights[:, g * 128 : (g + 1) * 128]
            block = kv_all[i // 2, pl.ds(lax.rem(i, 2) * 2, 2)].reshape(512, 256)
            return mixed + dot(weights.astype(BF16), block[:, HEAD_DIM:]), running

        zero = jnp.zeros((256, 128), F32)
        mixed, running = lax.fori_loop(0, 8, mix, (zero, zero), unroll=True)
        att_all[k, :, head_lanes] = (
            mixed / jnp.sum(running, axis=-1, keepdims=True)
        ).astype(BF16)
        copies = []
        for off in (1, 3, 2):
            copy = remote(att_all.at[k, :, head_lanes], att_all.at[k, :, head_lanes], at_x(off))
            start(copy)
            copies.append(copy)
        att_sends[k] = copies

    y_far = lax.rem(y + 2, NY)
    pairs, sum_far, sum_near = {}, {}, {}

    def chip_sum(k, to):
        return pair_own[k, to].astype(F32) + pair_in[k, to].astype(F32)

    def project(k):
        for copy in att_sends[k]:
            copy.wait_recv()
        rows = att_all[k]

        def other(i, carry):
            pair_out[k, i] = dot(rows, wo_all[2 * i + 1 - c]).astype(BF16)
            return carry

        lax.fori_loop(0, NY, other, 0, unroll=True)
        pairs[k] = remote(pair_out.at[k], pair_in.at[k], sibling)
        start(pairs[k])

        def mine(i, carry):
            pair_own[k, i] = dot(rows, wo_all[2 * i + c]).astype(BF16)
            return carry

        lax.fori_loop(0, NY, mine, 0, unroll=True)

    def send_sum(k):
        pairs[k].wait_recv()
        sum_out[k, y_far] = chip_sum(k, y_far).astype(BF16)
        sum_far[k] = {}
        for o in (1, 3):
            sum_far[k][o] = remote(
                sum_out.at[k, y_far, halves[o]], sum_mid.at[k, halves[o]], at_y(o)
            )
            start(sum_far[k][o])

    def pass_sum(k):
        sum_near[k] = {}
        for i, o in enumerate((1, 3)):
            to = lax.rem(y + o, NY)
            total = chip_sum(k, to)
            sum_far[k][o].wait_recv()
            passed = sum_mid[k, halves[o]].astype(F32)
            at = 0 if o == 1 else 128
            sum_out[k, to, halves[o]] = (total[at : at + 128] + passed).astype(BF16)
            rest = 128 - at
            sum_out[k, to, halves[4 - o]] = total[rest : rest + 128].astype(BF16)
            sum_near[k][o] = remote(sum_out.at[k, to], sum_in.at[k, i], at_y(o))
            start(sum_near[k][o])

    out_cols = pl.ds(pl.multiple_of(x * 256, 256), 256)
    gate_here = jnp.tanh(gate[:, out_cols])
    fin_sends = []
    first_fin = take(NX * 2)

    def finish(k):
        for o in (1, 3):
            sum_near[k][o].wait_recv()
        total = chip_sum(k, y) + sum_in[k, 0].astype(F32) + sum_in[k, 1].astype(F32)
        present = lax.broadcasted_iota(jnp.int32, (256, 256), 0) + k * 256 >= first_pos
        result = total * gate_here * jnp.where(present, 1.0, 0.0)
        fin_out[k] = result.astype(BF16)
        copy = pltpu.make_async_remote_copy(
            src_ref=fin_out.at[k], dst_ref=out.at[0, :, out_cols],
            send_sem=send_sems.at[first_fin + k], recv_sem=recv_sems.at[first_fin + NX + x],
            device_id=(z, k, m), device_id_type=pl.DeviceIdType.MESH,
        )
        keep = pltpu.make_async_copy(fin_out.at[k], out.at[0, :, out_cols], local_sems.at[6])

        @pl.when(x == k)
        def _():
            keep.start()

        @pl.when(x != k)
        def _():
            copy.start()

        fin_sends.append((copy, keep))

    attend(0)
    send_near(2)
    ring_start(ring_o, 3)
    send_near(3)
    attend(1)
    ring_wait(ring_o, 3)
    loads[5].wait()
    project(0)
    attend(2)
    send_sum(0)
    project(1)
    attend(3)
    pass_sum(0)
    send_sum(1)
    project(2)
    pass_sum(1)
    send_sum(2)
    project(3)
    finish(0)
    send_sum(3)
    pass_sum(2)
    finish(1)
    pass_sum(3)
    finish(2)
    finish(3)

    for off in (1, 3, 2):
        source = lax.rem(x - off + NX, NX)
        cols = pl.ds(pl.multiple_of(source * 256, 256), 256)
        pltpu.make_async_remote_copy(
            src_ref=fin_out.at[0], dst_ref=out.at[0, :, cols],
            send_sem=send_sems.at[first_fin], recv_sem=recv_sems.at[first_fin + NX + source],
            device_id=at_x(off), device_id_type=pl.DeviceIdType.MESH,
        ).wait_recv()
    for k, (copy, keep) in enumerate(fin_sends):

        @pl.when(x == k)
        def _():
            keep.wait()

        @pl.when(x != k)
        def _():
            copy.wait_send()

    for copy in sent:
        copy.wait_send()


def on_device(
    hidden, norm_gain, w_query, w_key, w_value, w_out, gate_alpha, latents, image_doc, image_pos
):
    vmem = pl.BlockSpec(memory_space=pltpu.VMEM)
    smem = pl.BlockSpec(memory_space=pltpu.SMEM)
    anywhere = pl.BlockSpec(memory_space=pl.ANY)
    buffer = pltpu.VMEM
    return pl.pallas_call(
        kernel,
        out_shape=jax.ShapeDtypeStruct((1, 256, 1024), BF16),
        in_specs=[
            anywhere, vmem, anywhere, anywhere, anywhere, anywhere, vmem, anywhere, smem, smem,
        ],
        out_specs=anywhere,
        scratch_shapes=[
            buffer((32, 8192), BF16),
            buffer((4, 16, 1280), BF16),
            buffer((1280, 512), BF16),
            buffer((1280, 512), BF16),
            buffer((NZ, 16, 1280), BF16),
            buffer((NM, NZ, 16, 1280), BF16),
            buffer((NX, 32, 2048), BF16),
            buffer((NX, NM, 32, 2048), BF16),
            buffer((NZ, 256, 512), BF16),
            buffer((NZ, 512, 256), BF16),
            buffer((NX, NY, 256, 256), BF16),
            buffer((NX, NY, 256, 256), BF16),
            buffer((NX * 2, 1, 128), jnp.int32),
            buffer((NX, NX, 256, 128), F32),
            buffer((NX, 256, 128), F32),
            buffer((NX, 2, 256, 128), F32),
            buffer((8, 256, 512), F32),
            buffer((NX, 256, 512), BF16),
            buffer((NX, NY, 256, 256), BF16),
            buffer((NX, NY, 256, 256), BF16),
            buffer((NX, NY, 256, 256), BF16),
            buffer((NX, NY, 256, 256), BF16),
            buffer((NX, 256, 256), BF16),
            buffer((NX, 2, 256, 256), BF16),
            buffer((NX, 256, 256), BF16),
            pltpu.SemaphoreType.DMA((160,)),
            pltpu.SemaphoreType.DMA((160,)),
            pltpu.SemaphoreType.DMA((8,)),
        ],
        compiler_params=pltpu.CompilerParams(
            collective_id=0, has_side_effects=True, vmem_limit_bytes=56 * 2**20
        ),
    )(
        hidden, norm_gain.reshape(1, -1), w_query, w_key, w_value, w_out,
        gate_alpha.reshape(1, -1), latents, image_doc.reshape(1, -1), image_pos.reshape(1, -1),
    )


def solution(mesh):
    placed = (
        P("dp", "seq", None),
        P(),
        P(("dp", "seq"), "mp"),
        P(None, "mp"),
        P(None, "mp"),
        P("mp", ("dp", "seq")),
        P("mp"),
        P(("dp", "seq"), None, None),
        P(),
        P(),
    )
    return jax.shard_map(
        on_device, mesh=mesh, in_specs=placed, out_specs=P("dp", "seq", "mp"), check_vma=False
    )
```
